32 devices in a mesh: seq: 8 (over z, x), chan: 4 (over y, core).
Axes of the slice: x: 2, y: 2, z: 4, core: 2. Of those that a mesh axis runs over, the one named last changes fastest.
Arguments:
- token_ids: int32 [2048], P('seq'), may hold values from 0 to 511
- embed_table: bfloat16 [512, 8192], P(None, 'chan'), may hold values from -6 to 6
- se_query: bfloat16 [2048, 8192], P('seq', 'chan'), may hold values from -3 to 3
- se_key: bfloat16 [2048, 8192], P('seq', 'chan'), may hold values from -6 to 6
- se_filter: bfloat16 [512, 7], P('chan'), may hold values from -2 to 2
- mr_query: bfloat16 [2048, 8192], P('seq', 'chan'), may hold values from -3 to 3
- mr_key: bfloat16 [2048, 8192], P('seq', 'chan'), may hold values from -6 to 6
- mr_filter: bfloat16 [512, 128], P('chan'), may hold values from -0.5 to 0.5
- li_query: bfloat16 [2048, 8192], P('seq', 'chan'), may hold values from -3 to 3
- li_key: bfloat16 [2048, 8192], P('seq', 'chan'), may hold values from -6 to 6
- li_rate: float32 [512, 16], P('chan'), may hold values from 4.8828124e-06 to 0.05
- li_residue: float32 [512, 16], P('chan'), may hold values from -1.5 to 1.5
- attn_query: bfloat16 [2048, 8192], P('seq', 'chan'), may hold values from -7 to 7
- attn_key: bfloat16 [2048, 8192], P('seq', 'chan'), may hold values from -7 to 7
Outputs:
- block_out: bfloat16 [2048, 8192], P('seq', 'chan')
The draws below stay inside these ranges and needn't reach their ends.
All inputs are finite; a program needn't handle non-finite values.
Results may differ from the reference program's by a relative error of at most 0.01.
Values may be sent and summed in bfloat16 or wider, within the bound.
A program may use at most 192 MiB of HBM per device.

```python
import math
import jax
import jax.numpy as jnp
import numpy as np
from jax import lax

D = 8192
HEAD_DIM = 128
VOCAB = 512
GROUP_CH = 16
SE_LEN = 7
MR_LEN = 128
STATE = 16
TOTAL = 2048
HEADS = 64
GROUPS = 512


def attention_pair(key):
    query_seed = jax.random.fold_in(key, 101)
    key_seed = jax.random.fold_in(key, 202)
    queries = jnp.clip(1.5 * jax.random.normal(query_seed, (TOTAL, D), jnp.float32), -7.0, 7.0)
    keys_drawn = jnp.clip(1.5 * jax.random.normal(key_seed, (TOTAL, D), jnp.float32), -7.0, 7.0)
    return (queries, keys_drawn)


def draw_attn_query(key, part):
    return attention_pair(key)[0].astype(jnp.bfloat16)


def draw_attn_key(key, part):
    return attention_pair(key)[1].astype(jnp.bfloat16)


def with_ends(values, key, smallest, top_value):
    longest = values.shape.index(max(values.shape))
    spots = []
    for shift in (0, 1):
        where = [jax.random.randint(jax.random.fold_in(key, axis), (), 0, length) for axis, length in enumerate(values.shape)]
        where[longest] = (where[longest] + shift) % values.shape[longest]
        spots.append(tuple(where))
    return values.at[spots[0]].set(smallest).at[spots[1]].set(top_value)


def shard_levels(rng, extent, cuts, low, largest):
    level, own = 1.0, jax.random.fold_in(rng, 6)
    for position, parts in cuts:
        draws = jnp.exp(jax.random.uniform(jax.random.fold_in(own, position), (parts,), jnp.float32, low / len(cuts), largest / len(cuts)))
        level = level * jnp.repeat(draws, extent[position] // parts).reshape([-1 if axis == position else 1 for axis in range(len(extent))])
    return level


def cumulative_ranks(amount, lean):
    loads = [(1 << 20) // math.isqrt(standing ** lean) + 1 for standing in range(1, amount + 1)]
    spread = 1 + sum(loads) // (1 << 30)
    return np.cumsum(np.array([max(1, weight // spread) for weight in loads]))


def skewed_ids(rng, extent, count, slope):
    grid = cumulative_ranks(count, slope)
    lot = jax.random.randint(jax.random.fold_in(rng, 1), extent, 0, int(grid[count - 1]))
    grade = jnp.searchsorted(jnp.asarray(grid, jnp.int32), lot, side="right")
    return jax.random.permutation(jax.random.fold_in(rng, 2), count)[grade].astype(jnp.int32)


def normal_values(stream_key, shape, deviation, most, shards=(), kind=jnp.bfloat16):
    level = shard_levels(stream_key, shape, shards, -0.22, 0.18) if shards else 1.0
    values = jax.random.normal(stream_key, shape, jnp.float32) * deviation * level
    return jnp.minimum(jnp.maximum(values, -most), most).astype(kind)


def setup_inputs(seed: int = 0) -> dict:
    key_of = jax.random.split(jax.random.key(seed), 15)
    return {
        "token_ids": with_ends(skewed_ids(key_of[0], (TOTAL,), VOCAB, 2), jax.random.fold_in(key_of[0], 3), 0, VOCAB - 1).astype(jnp.int32),
        "embed_table": normal_values(key_of[1], (VOCAB, D), 1.0, 6.0, ((1, 4),)),
        "se_query": normal_values(key_of[2], (TOTAL, D), 0.5, 3.0, ((0, 8), (1, 4))),
        "se_key": normal_values(key_of[3], (TOTAL, D), 1.0, 6.0, ((0, 8), (1, 4))),
        "se_filter": normal_values(key_of[4], (GROUPS, SE_LEN), SE_LEN ** -0.5, 2.0, ((0, 4),)),
        "mr_query": normal_values(key_of[5], (TOTAL, D), 0.5, 3.0, ((0, 8), (1, 4))),
        "mr_key": normal_values(key_of[6], (TOTAL, D), 1.0, 6.0, ((0, 8), (1, 4))),
        "mr_filter": normal_values(key_of[7], (GROUPS, MR_LEN), MR_LEN ** -0.5, 0.5, ((0, 4),)),
        "li_query": normal_values(key_of[8], (TOTAL, D), 0.5, 3.0, ((0, 8), (1, 4))),
        "li_key": normal_values(key_of[9], (TOTAL, D), 1.0, 6.0, ((0, 8), (1, 4))),
        "li_rate": jnp.clip(jnp.exp(math.log(0.05) - 9.2340569 * jax.random.uniform(key_of[10], (GROUPS, STATE), jnp.float32) ** shard_levels(key_of[10], (GROUPS, STATE), ((0, 4),), -0.2, 0.2)), 4.882812390860636e-06, 0.05),
        "li_residue": normal_values(key_of[11], (GROUPS, STATE), 0.25, 1.5, ((0, 4),), jnp.float32),
        "attn_query": draw_attn_query(jax.random.fold_in(key_of[14], 71), 0),
        "attn_key": draw_attn_key(jax.random.fold_in(key_of[14], 71), 0),
    }


def grouped_conv(signal, filters):
    tap_count = filters.shape[1]
    row_total = signal.shape[0]
    tap_weights = jnp.repeat(filters.astype(jnp.float32), GROUP_CH, axis=0)
    padded = jnp.concatenate([jnp.zeros((tap_count - 1, signal.shape[1]), jnp.float32), signal.astype(jnp.float32)], 0)

    def add_tap(tap_index, running):
        start_row = (tap_count - 1 - tap_index).astype(jnp.int32)
        window = lax.dynamic_slice_in_dim(padded, start_row, row_total, 0)
        column = lax.dynamic_index_in_dim(tap_weights, tap_index.astype(jnp.int32), 1, keepdims=False)
        return running + window * column[None, :]
    return lax.fori_loop(0, tap_count, add_tap, jnp.zeros((row_total, signal.shape[1]), jnp.float32))

def gated_layer(stream, out_gate, in_gate, filters):
    gated_in = (in_gate.astype(jnp.float32) * stream.astype(jnp.float32)).astype(jnp.bfloat16)
    conv_out = grouped_conv(gated_in, filters)
    return (stream.astype(jnp.float32) + out_gate.astype(jnp.float32) * conv_out).astype(jnp.bfloat16)

def modal_layer(stream, out_gate, in_gate, li_rate, li_residue):
    gated_in = (in_gate.astype(jnp.float32) * stream.astype(jnp.float32)).astype(jnp.bfloat16)
    gain = li_residue * jnp.sqrt(1.0 - jnp.exp(-2.0 * li_rate) + 1.0 / TOTAL)
    decay_ch = jnp.repeat(jnp.exp(-li_rate), GROUP_CH, axis=0).T
    gain_ch = jnp.repeat(gain, GROUP_CH, axis=0).T

    def advance(state, row_vals):
        state = decay_ch * state + row_vals[None, :]
        return (state, lax.optimization_barrier(jnp.sum(gain_ch * state, axis=0)))
    _, conv_out = lax.scan(advance, jnp.zeros((STATE, D), jnp.float32), gated_in.astype(jnp.float32))
    return (stream.astype(jnp.float32) + out_gate.astype(jnp.float32) * conv_out).astype(jnp.bfloat16)

def reference(token_ids, embed_table, se_query, se_key, se_filter, mr_query, mr_key, mr_filter, li_query, li_key, li_rate, li_residue, attn_query, attn_key):
    stream = embed_table[token_ids]
    stream = gated_layer(stream, se_query, se_key, se_filter)
    stream = gated_layer(stream, mr_query, mr_key, mr_filter)
    stream = modal_layer(stream, li_query, li_key, li_rate, li_residue)
    scale = HEAD_DIM ** (-0.5)
    positions = jnp.arange(TOTAL, dtype=jnp.int32)
    allowed = positions[None, :] <= positions[:, None]
    head_q = attn_query.reshape(TOTAL, HEADS, HEAD_DIM).transpose(1, 0, 2)
    head_k = attn_key.reshape(TOTAL, HEADS, HEAD_DIM).transpose(1, 0, 2)
    head_v = stream.reshape(TOTAL, HEADS, HEAD_DIM).transpose(1, 0, 2)

    def one_head(packed):
        query_h, key_h, value_h = packed
        scores = jnp.dot(query_h.astype(jnp.float32), key_h.astype(jnp.float32).T, precision=lax.Precision.HIGHEST) * scale
        scores = jnp.where(allowed, scores, -1e+30)
        peak = lax.optimization_barrier(jnp.max(scores, axis=1, keepdims=True))
        weights = jnp.where(allowed, jnp.exp(scores - peak), 0.0)
        totals = lax.optimization_barrier(jnp.sum(weights, axis=1))
        weights_low = weights.astype(jnp.bfloat16)
        mixed = jnp.dot(weights_low.astype(jnp.float32), value_h.astype(jnp.float32), precision=lax.Precision.HIGHEST)
        return (mixed / totals[:, None]).astype(jnp.bfloat16)
    attended = lax.map(one_head, (head_q, head_k, head_v))
    attended = attended.transpose(1, 0, 2).reshape(TOTAL, D)
    return (stream.astype(jnp.float32) + attended.astype(jnp.float32)).astype(jnp.bfloat16)
```

```python
import functools
import jax
import jax.numpy as jnp
from jax import lax
from jax.experimental import pallas as pl
from jax.experimental.pallas import tpu as pltpu
from jax.sharding import PartitionSpec as P

HEAD_DIM = 128


HIGHEST = lax.Precision.HIGHEST


def from_behind(block, axis, distance):
    devices = range(lax.axis_size(axis))
    route = [(i - distance, i) for i in devices if i - distance in devices]
    return lax.ppermute(block, axis, route)


def carried_in(value, axis, combine, identity):
    count, here = (lax.axis_size(axis), lax.axis_index(axis))
    everything = jax.tree.map(lambda part: lax.all_gather(part, axis), value)
    start = jax.tree.map(
        lambda part, zero: jnp.broadcast_to(jnp.asarray(zero, part.dtype), part.shape),
        value,
        identity,
    )

    def step(k, before):
        reached = k < here
        new = combine(before, jax.tree.map(lambda part: part[k], everything))
        return jax.tree.map(lambda a, b: jnp.where(reached, a, b), new, before)

    return lax.fori_loop(0, count, step, start)


def toeplitz_tables(filters, taps):
    lag_grid = (
        jnp.arange(taps, dtype=jnp.int32)[:, None] - jnp.arange(taps, dtype=jnp.int32)[None, :]
    )
    tap_ids = jnp.arange(taps, dtype=jnp.int32)[:, None, None]
    near_select = (lag_grid[None] == tap_ids).astype(jnp.float32)
    far_select = ((lag_grid + taps)[None] == tap_ids).astype(jnp.float32)
    filters_f = filters.astype(jnp.float32)
    current = jnp.einsum("gk,kts->gts", filters_f, near_select, precision=HIGHEST)
    previous = jnp.einsum("gk,kts->gts", filters_f, far_select, precision=HIGHEST)
    return (current, previous)


def local(
    token_ids,
    embed_table,
    se_query,
    se_key,
    se_filter,
    mr_query,
    mr_key,
    mr_filter,
    li_query,
    li_key,
    li_rate,
    li_residue,
    attn_query,
    attn_key,
):
    f32 = jnp.float32
    bf16 = jnp.bfloat16
    row_count = token_ids.shape[0]
    channels = embed_table.shape[1]
    group_count = se_filter.shape[0]
    group_width = channels // group_count
    seq_count = lax.axis_size("seq")
    chan_count = lax.axis_size("chan")
    total_len = row_count * seq_count
    vocab_ids = jnp.arange(embed_table.shape[0], dtype=jnp.int32)
    one_hot = (token_ids[:, None] == vocab_ids[None, :]).astype(bf16)
    stream = jnp.dot(one_hot, embed_table, preferred_element_type=f32).astype(bf16)
    se_taps = se_filter.shape[1]
    se_input = (se_key.astype(f32) * stream.astype(f32)).astype(bf16)
    se_edge = from_behind(se_input[row_count - (se_taps - 1) :], "seq", 1)
    se_padded = jnp.concatenate([se_edge, se_input], 0)
    tap_weights = jnp.repeat(se_filter.astype(f32), group_width, axis=0)
    se_conv = jnp.zeros((row_count, channels), f32)
    for tap_index in range(se_taps):
        start_row = se_taps - 1 - tap_index
        se_conv = (
            se_conv
            + se_padded[start_row : start_row + row_count].astype(f32) * tap_weights[:, tap_index]
        )
    stream = (stream.astype(f32) + se_query.astype(f32) * se_conv).astype(bf16)
    mr_taps = mr_filter.shape[1]
    mr_input = (mr_key.astype(f32) * stream.astype(f32)).astype(bf16)
    mr_edge = from_behind(mr_input[row_count - (mr_taps - 1) :], "seq", 1)
    block_count = row_count // mr_taps
    extended = jnp.concatenate([jnp.zeros((1, channels), bf16), mr_edge, mr_input], 0)
    extended = extended.reshape(block_count + 1, mr_taps, group_count, group_width)
    current_f, previous_f = toeplitz_tables(mr_filter, mr_taps)
    current = current_f.astype(bf16)
    previous = previous_f.astype(bf16)
    mr_conv = jnp.einsum("gts,bsgc->btgc", current, extended[1:], preferred_element_type=f32)
    mr_conv = mr_conv + jnp.einsum(
        "gts,bsgc->btgc", previous, extended[:-1], preferred_element_type=f32
    )
    stream = (
        stream.astype(f32) + mr_query.astype(f32) * mr_conv.reshape(row_count, channels)
    ).astype(bf16)
    li_input = (li_key.astype(f32) * stream.astype(f32)).astype(bf16)
    gain = li_residue * jnp.sqrt(1.0 - jnp.exp(-2.0 * li_rate) + 1.0 / total_len)
    lag_values = jnp.arange(mr_taps, dtype=f32)
    kernel_rows = jnp.sum(gain[:, :, None] * jnp.exp(-li_rate[:, :, None] * lag_values), axis=1)
    intra, unused_far = toeplitz_tables(kernel_rows, mr_taps)
    blocks_f = li_input.astype(f32).reshape(block_count, mr_taps, group_count, group_width)
    local_conv = jnp.einsum("gts,bsgc->btgc", intra, blocks_f, precision=HIGHEST)
    to_end = jnp.exp(-li_rate[:, :, None] * (mr_taps - 1 - lag_values))
    block_states = jnp.einsum("gms,bsgc->bmgc", to_end, blocks_f, precision=HIGHEST)
    block_ids = jnp.arange(block_count, dtype=f32)
    tail_decay = jnp.exp(-li_rate[None] * (mr_taps * (block_count - 1 - block_ids))[:, None, None])
    shard_state = jnp.einsum("bgm,bmgc->mgc", tail_decay, block_states, precision=HIGHEST)
    rate_column = li_rate.T[:, :, None]
    shard_decay = jnp.exp(-rate_column * row_count)

    def combine(earlier, later):
        return (earlier[0] * later[0], earlier[1] * later[0] + later[1])

    prefix = carried_in(
        (shard_decay, shard_state),
        "seq",
        combine,
        (jnp.ones_like(shard_decay), jnp.zeros_like(shard_state)),
    )
    carry_in = prefix[1]
    block_lag = block_ids[:, None] - 1.0 - block_ids[None, :]
    mixing = jnp.exp(
        -li_rate[None, None] * (mr_taps * jnp.maximum(block_lag, 0.0))[:, :, None, None]
    )
    mixing = jnp.where(block_lag[:, :, None, None] >= 0, mixing, 0.0)
    lead_decay = jnp.exp(-li_rate[None] * (mr_taps * block_ids)[:, None, None])
    block_carry = jnp.einsum("bdgm,dmgc->bmgc", mixing, block_states, precision=HIGHEST)
    block_carry = block_carry + jnp.einsum("bgm,mgc->bmgc", lead_decay, carry_in, precision=HIGHEST)
    emit = gain[:, None, :] * jnp.exp(-li_rate[:, None, :] * (lag_values + 1.0)[None, :, None])
    carry_conv = jnp.einsum("gtm,bmgc->btgc", emit, block_carry, precision=HIGHEST)
    li_conv = (local_conv + carry_conv).reshape(row_count, channels)
    stream = (stream.astype(f32) + li_query.astype(f32) * li_conv).astype(bf16)
    head_dim = HEAD_DIM
    local_heads = channels // head_dim
    part_rows = row_count // chan_count
    chan_index = lax.axis_index("chan")
    queries = attn_query.reshape(row_count, local_heads, head_dim)
    keys_local = attn_key.reshape(row_count, local_heads, head_dim)
    values_local = stream.reshape(row_count, local_heads, head_dim)
    q_heads, k_heads, v_heads = (
        lax.all_to_all(
            lax.all_to_all(queries, "chan", split_axis=0, concat_axis=1, tiled=True),
            "seq",
            split_axis=1,
            concat_axis=0,
            tiled=True,
        ),
        lax.all_to_all(
            lax.all_to_all(keys_local, "chan", split_axis=0, concat_axis=1, tiled=True),
            "seq",
            split_axis=1,
            concat_axis=0,
            tiled=True,
        ),
        lax.all_to_all(
            lax.all_to_all(values_local, "chan", split_axis=0, concat_axis=1, tiled=True),
            "seq",
            split_axis=1,
            concat_axis=0,
            tiled=True,
        ),
    )
    k_all, v_all = (
        lax.all_gather(k_heads, "chan", axis=0, tiled=True),
        lax.all_gather(v_heads, "chan", axis=0, tiled=True),
    )
    key_index = jnp.arange(chan_count * seq_count * part_rows, dtype=jnp.int32)
    key_chan = key_index // (seq_count * part_rows)
    key_rest = key_index % (seq_count * part_rows)
    key_pos = key_rest // part_rows * row_count + key_chan * part_rows + key_rest % part_rows
    query_count = q_heads.shape[0]
    head_count = q_heads.shape[1]
    query_index = jnp.arange(query_count, dtype=jnp.int32)
    query_pos = (
        query_index // part_rows * row_count + chan_index * part_rows + query_index % part_rows
    )
    block_rows = 512
    scale = head_dim ** (-0.5)

    def attend_block(packed):
        query_block, pos_block = packed
        scores = jnp.einsum("qhd,khd->hqk", query_block, k_all, preferred_element_type=f32) * scale
        allowed = key_pos[None, :] <= pos_block[:, None]
        scores = jnp.where(allowed[None], scores, -1e30)
        peak = jnp.max(scores, axis=2, keepdims=True)
        weights = jnp.where(allowed[None], jnp.exp(scores - peak), 0.0)
        totals = jnp.sum(weights, axis=2)
        mixed = jnp.einsum("hqk,khd->qhd", weights.astype(bf16), v_all, preferred_element_type=f32)
        return (mixed / totals.T[:, :, None]).astype(bf16)

    attended = lax.map(
        attend_block,
        (
            q_heads.reshape(query_count // block_rows, block_rows, head_count, head_dim),
            query_pos.reshape(query_count // block_rows, block_rows),
        ),
    )
    attended = attended.reshape(query_count, head_count, head_dim)
    returned = lax.all_to_all(
        lax.all_to_all(attended, "seq", split_axis=0, concat_axis=1, tiled=True),
        "chan",
        split_axis=1,
        concat_axis=0,
        tiled=True,
    )
    return (stream.astype(f32) + returned.reshape(row_count, channels).astype(f32)).astype(bf16)


LANES = 128
HALO = 16
MESH = pl.DeviceIdType.MESH


def fused(
    n, total_len,
    ids_ref, table_ref, sq_ref, sk_ref, sw_ref, mq_ref, mk_ref, mf_ref, lq_ref, lk_ref,
    rate_ref, res_ref, q_hbm, k_hbm, out_hbm,
    st, xs, hs, hx, mx, lx, lc, wt, s_mine, s_all, qh, kh, vh, ob, vb,
    qss, qrs, kss, krs, vss, vrs, oss, ors, hss, hrs, sss, srs, own,
):
    f32, bf16 = jnp.float32, jnp.bfloat16
    me = lax.axis_index("seq")
    rows, chans = sq_ref.shape
    tiles = chans // LANES
    width = chans // n
    per = width // LANES
    half = rows // 2
    groups = mf_ref.shape[0]
    gpt = groups // tiles
    gw = LANES // gpt
    modes = LANES // gpt
    taps = sw_ref.shape[0]

    def lanes(start, size):
        return pl.ds(pl.multiple_of(start, LANES), size)

    def block(i):
        return pl.ds(pl.multiple_of(i * rows, rows), rows)

    barrier = pltpu.get_barrier_semaphore()

    def greet(i, c):
        pl.semaphore_signal(
            barrier, inc=1, device_id={"seq": lax.rem(me + i, n)}, device_id_type=MESH
        )
        return c

    lax.fori_loop(1, n, greet, 0)
    pl.semaphore_wait(barrier, n - 1)

    def spread(src, dst, ss, rs, peer, owner):
        return pltpu.make_async_remote_copy(
            src_ref=src.at[:, lanes(peer * width, width)],
            dst_ref=dst.at[block(owner), :],
            send_sem=ss.at[peer], recv_sem=rs.at[owner],
            device_id={"seq": peer}, device_id_type=MESH,
        )

    def give_back(peer, owner):
        return pltpu.make_async_remote_copy(
            src_ref=ob.at[block(peer), :],
            dst_ref=out_hbm.at[:, lanes(owner * width, width)],
            send_sem=oss.at[peer], recv_sem=ors.at[owner],
            device_id={"seq": peer}, device_id_type=MESH,
        )

    def state_copy(peer, owner):
        return pltpu.make_async_remote_copy(
            src_ref=s_mine, dst_ref=s_all.at[owner],
            send_sem=sss.at[peer], recv_sem=srs.at[owner],
            device_id={"seq": peer}, device_id_type=MESH,
        )

    nxt = lax.rem(me + 1, n)
    se_halo = pltpu.make_async_remote_copy(
        src_ref=hs, dst_ref=hx, send_sem=hss.at[0], recv_sem=hrs.at[0],
        device_id={"seq": nxt}, device_id_type=MESH,
    )
    mr_halo = pltpu.make_async_remote_copy(
        src_ref=mx.at[pl.ds(rows, half), :], dst_ref=mx.at[pl.ds(0, half), :],
        send_sem=hss.at[1], recv_sem=hrs.at[1],
        device_id={"seq": nxt}, device_id_type=MESH,
    )

    def send_all(src, dst, ss, rs):
        def one(i, c):
            spread(src, dst, ss, rs, lax.rem(me + i, n), me).start()
            return c

        lax.fori_loop(1, n, one, 0)

    own_q = pltpu.make_async_copy(q_hbm.at[:, lanes(me * width, width)], qh.at[block(me), :], own.at[0])
    own_k = pltpu.make_async_copy(k_hbm.at[:, lanes(me * width, width)], kh.at[block(me), :], own.at[1])
    own_q.start()
    own_k.start()

    def iota(shape, dim):
        return lax.broadcasted_iota(jnp.int32, shape, dim)

    vocab = table_ref.shape[0]
    ids_row = jnp.broadcast_to(ids_ref[...], (rows, rows))
    eye = iota((rows, rows), 0) == iota((rows, rows), 1)
    ids_col = jnp.sum(jnp.where(eye, ids_row, 0.0), axis=1, keepdims=True).astype(jnp.int32)
    one_hot = (iota((rows, vocab), 1) == ids_col).astype(f32).astype(bf16)

    def embed(j, c):
        at = lanes(j * 2 * LANES, 2 * LANES)
        e = jnp.dot(one_hot, table_ref[:, at], preferred_element_type=f32)
        st[:, at] = e.astype(bf16)
        gated = (sk_ref[:, at].astype(f32) * e).astype(bf16)
        xs[pl.ds(HALO, rows), at] = gated.astype(f32)
        hs[:, at] = gated[rows - HALO :, :]
        return c

    lax.fori_loop(0, tiles // 2, embed, 0)

    @pl.when(me < n - 1)
    def _():
        se_halo.start()

    send_all(q_hbm, qh, qss, qrs)

    @pl.when(me > 0)
    def _():
        se_halo.wait_recv()

    @pl.when(me == 0)
    def _():
        hx[...] = jnp.zeros_like(hx)
        mx[pl.ds(0, half), :] = jnp.zeros((half, chans), bf16)

    def short(j, c):
        at = lanes(j * LANES, LANES)
        xs[pl.ds(0, HALO), at] = hx[:, at].astype(f32)
        conv = jnp.zeros((rows, LANES), f32)
        for k in range(taps):
            conv = conv + xs[pl.ds(HALO - k, rows), at] * sw_ref[pl.ds(k, 1), at]
        s1 = (st[:, at].astype(f32) + sq_ref[:, at].astype(f32) * conv).astype(bf16)
        st[:, at] = s1
        mx[pl.ds(half, rows), at] = (mk_ref[:, at].astype(f32) * s1.astype(f32)).astype(bf16)
        return c

    lax.fori_loop(0, tiles, short, 0)

    @pl.when(me < n - 1)
    def _():
        mr_halo.start()

    send_all(k_hbm, kh, kss, krs)

    @pl.when(me > 0)
    def _():
        mr_halo.wait_recv()

    eye_l = iota((LANES, LANES), 0) == iota((LANES, LANES), 1)
    lane_group = iota((half, 2 * LANES), 1) % LANES // gw
    back = (rows - 1 - iota((LANES, rows), 1)).astype(f32)
    causal = iota((half, rows), 1) <= iota((half, rows), 0) + half

    def column(row):
        return jnp.sum(
            jnp.where(eye_l, jnp.broadcast_to(row, (LANES, LANES)), 0.0), axis=1, keepdims=True
        )

    def gain_of(j):
        rate = rate_ref[pl.ds(j, 1), :]
        return rate, res_ref[pl.ds(j, 1), :] * jnp.sqrt(
            1.0 - jnp.exp(-2.0 * rate) + 1.0 / total_len
        )

    def pick(values, height, lg):
        acc = values[0:height, :]
        for g in range(1, gpt):
            acc = jnp.where(lg == g, values[g * height : (g + 1) * height, :], acc)
        return acc

    def toeplitz(kernels, mask):
        for g in range(gpt):
            wide = jnp.broadcast_to(kernels[g : g + 1, :], (half, rows))
            rolled = pltpu.roll(wide, half + 1, 1, stride=1, stride_axis=0)
            if mask is not None:
                rolled = jnp.where(mask, rolled, 0.0)
            wt[pl.ds(g * half, half), :] = rolled.astype(bf16)

    def stack(acc):
        return jnp.concatenate([acc[:, :LANES], acc[:, LANES:]], axis=0)

    lane_group_m = iota((modes, LANES), 1) // gw

    def medium(j, c):
        at = lanes(j * LANES, LANES)
        toeplitz(mf_ref[pl.ds(pl.multiple_of(j * gpt, gpt), gpt), :], None)
        both = jnp.concatenate([mx[pl.ds(0, rows), at], mx[pl.ds(half, rows), at]], axis=1)
        conv = stack(
            pick(jnp.dot(wt[...], both, preferred_element_type=f32), half, lane_group)
        )
        s2 = (st[:, at].astype(f32) + mq_ref[:, at].astype(f32) * conv).astype(bf16)
        st[:, at] = s2
        gated = (lk_ref[:, at].astype(f32) * s2.astype(f32)).astype(bf16)
        lx[:, at] = gated
        fade = jnp.exp(-column(rate_ref[pl.ds(j, 1), :]) * back).astype(bf16)
        ends = jnp.dot(fade, gated, preferred_element_type=f32)
        s_mine[:, at] = pick(ends, modes, lane_group_m).astype(bf16)
        return c

    lax.fori_loop(0, tiles, medium, 0)

    def push_state(p, c):
        state_copy(p, me).start()
        return c

    lax.fori_loop(me + 1, n, push_state, 0)

    def long_local(j, c):
        at = lanes(j * LANES, LANES)
        rate, gain = gain_of(j)
        fade = jnp.exp(-column(rate) * back) * column(gain)
        toeplitz(jnp.sum(fade.reshape(gpt, modes, rows), axis=1), causal)
        x = lx[:, at]
        first = jnp.concatenate([jnp.zeros((half, LANES), bf16), x[:half, :]], axis=0)
        both = jnp.concatenate([first, x], axis=1)
        lc[:, at] = stack(
            pick(jnp.dot(wt[...], both, preferred_element_type=f32), half, lane_group)
        )
        return c

    lax.fori_loop(0, tiles, long_local, 0)

    def take_state(p, c):
        state_copy(me, p).wait_recv()
        return c

    lax.fori_loop(0, me, take_state, 0)

    after = (iota((rows, LANES), 0) + 1).astype(f32)
    same = iota((LANES, LANES), 0) // modes == iota((LANES, LANES), 1) // gw

    def long_carry(i, c):
        d = lax.rem(me + 1 + i, n)
        for u in range(per):
            j = d * per + u
            at = lanes(j * LANES, LANES)
            rate, gain = gain_of(j)
            rate_m = pick(jnp.broadcast_to(column(rate), (LANES, LANES)), modes, lane_group_m)
            decay = jnp.exp(-rate_m * float(rows))
            carry = lax.fori_loop(
                0, me, lambda p, s: s * decay + s_all[p, :, at].astype(f32),
                jnp.zeros((modes, LANES), f32),
            )
            full = jnp.where(same, jnp.concatenate([carry] * gpt, axis=0), 0.0)
            high = full.astype(bf16)
            low = (full - high.astype(f32)).astype(bf16)
            emit = (gain * jnp.exp(-after * rate)).astype(bf16)
            conv = lc[:, at] + jnp.dot(
                jnp.concatenate([emit, emit], axis=1),
                jnp.concatenate([high, low], axis=0),
                preferred_element_type=f32,
            )
            vb[:, at] = (st[:, at].astype(f32) + lq_ref[:, at].astype(f32) * conv).astype(bf16)

        @pl.when(i < n - 1)
        def _():
            spread(vb, vh, vss, vrs, d, me).start()

        return c

    lax.fori_loop(0, n, long_carry, 0)
    own_v = pltpu.make_async_copy(vb.at[:, lanes(me * width, width)], vh.at[block(me), :], own.at[2])
    own_v.start()
    own_q.wait()
    own_k.wait()
    own_v.wait()

    def arrived(i, c):
        p = lax.rem(me + n - i, n)
        spread(q_hbm, qh, qss, qrs, me, p).wait_recv()
        spread(k_hbm, kh, kss, krs, me, p).wait_recv()
        spread(vb, vh, vss, vrs, me, p).wait_recv()
        return c

    lax.fori_loop(1, n, arrived, 0)

    factor = HEAD_DIM ** (-0.5) * 1.4426950408889634
    below = iota((rows, rows), 1) <= iota((rows, rows), 0)

    def attend(i, c):
        r = lax.rem(me + 1 + i, n)
        qs = [qh[block(r), u * LANES : (u + 1) * LANES] for u in range(per)]

        def part(b, state, masked):
            new = []
            for u in range(per):
                peak, total, acc = state[u]
                cols = slice(u * LANES, (u + 1) * LANES)
                s = lax.dot_general(
                    qs[u], kh[block(b), cols], (((1,), (1,)), ((), ())), preferred_element_type=f32
                ) * factor
                if masked:
                    s = jnp.where(below, s, -1e30)
                top = jnp.maximum(peak, jnp.max(s, axis=1, keepdims=True))
                w = jnp.exp2(s - top)
                shrink = jnp.exp2(peak - top)
                total = total * shrink + jnp.sum(w, axis=1, keepdims=True)
                acc = acc * shrink + jnp.dot(
                    w.astype(bf16), vh[block(b), cols], preferred_element_type=f32
                )
                new.append((top, total, acc))
            return tuple(new)

        start = tuple(
            (jnp.full((rows, 1), -1e30, f32), jnp.zeros((rows, 1), f32), jnp.zeros((rows, LANES), f32))
            for u in range(per)
        )
        state = part(r, start, True)
        state = lax.fori_loop(0, r, lambda b, s: part(b, s, False), state)
        for u in range(per):
            peak, total, acc = state[u]
            cols = slice(u * LANES, (u + 1) * LANES)
            got = (acc / total).astype(bf16)
            ob[block(r), cols] = (vh[block(r), cols].astype(f32) + got.astype(f32)).astype(bf16)

        @pl.when(i < n - 1)
        def _():
            give_back(r, me).start()

        return c

    lax.fori_loop(0, n, attend, 0)
    own_o = pltpu.make_async_copy(ob.at[block(me), :], out_hbm.at[:, lanes(me * width, width)], own.at[3])
    own_o.start()

    @pl.when(me < n - 1)
    def _():
        se_halo.wait_send()
        mr_halo.wait_send()

    def sent_state(p, c):
        state_copy(p, me).wait_send()
        return c

    lax.fori_loop(me + 1, n, sent_state, 0)

    def finish(i, c):
        p = lax.rem(me + i, n)
        spread(q_hbm, qh, qss, qrs, p, me).wait_send()
        spread(k_hbm, kh, kss, krs, p, me).wait_send()
        spread(vb, vh, vss, vrs, p, me).wait_send()
        give_back(p, me).wait_send()
        give_back(me, p).wait_recv()
        return c

    lax.fori_loop(1, n, finish, 0)
    own_o.wait()


def by_heads(
    token_ids, embed_table, se_query, se_key, se_filter, mr_query, mr_key, mr_filter,
    li_query, li_key, li_rate, li_residue, attn_query, attn_key,
):
    f32, bf16 = jnp.float32, jnp.bfloat16
    n = lax.axis_size("seq")
    rows, chans = se_query.shape
    groups, mr_taps = mr_filter.shape
    tiles = chans // LANES
    width = chans // n
    group_width = chans // groups
    modes = li_rate.shape[1]
    short_taps = jnp.repeat(se_filter.astype(f32).T, group_width, axis=1)
    reversed_mr = jnp.concatenate(
        [jnp.zeros((groups, rows - mr_taps), f32), mr_filter.astype(f32)[:, ::-1]], axis=1
    )
    vmem = pl.BlockSpec(memory_space=pltpu.VMEM)
    anywhere = pl.BlockSpec(memory_space=pl.ANY)
    dma = pltpu.SemaphoreType.DMA
    return pl.pallas_call(
        functools.partial(fused, n, n * rows),
        out_shape=jax.ShapeDtypeStruct((rows, chans), bf16),
        in_specs=[vmem] * 12 + [anywhere] * 2,
        out_specs=anywhere,
        scratch_shapes=[
            pltpu.VMEM((rows, chans), bf16),
            pltpu.VMEM((rows + HALO, chans), f32),
            pltpu.VMEM((HALO, chans), bf16),
            pltpu.VMEM((HALO, chans), bf16),
            pltpu.VMEM((rows + rows // 2, chans), bf16),
            pltpu.VMEM((rows, chans), bf16),
            pltpu.VMEM((rows, chans), f32),
            pltpu.VMEM((groups // tiles * rows // 2, rows), bf16),
            pltpu.VMEM((modes, chans), bf16),
            pltpu.VMEM((n, modes, chans), bf16),
            pltpu.VMEM((n * rows, width), bf16),
            pltpu.VMEM((n * rows, width), bf16),
            pltpu.VMEM((n * rows, width), bf16),
            pltpu.VMEM((n * rows, width), bf16),
            pltpu.VMEM((rows, chans), bf16),
        ]
        + [dma((n,))] * 8 + [dma((2,))] * 2 + [dma((n,))] * 2 + [dma((4,))],
        compiler_params=pltpu.CompilerParams(
            collective_id=0, has_side_effects=True, vmem_limit_bytes=52 * 2**20
        ),
    )(
        token_ids.astype(f32).reshape(1, rows), embed_table, se_query, se_key, short_taps,
        mr_query, mr_key, reversed_mr, li_query, li_key,
        li_rate.reshape(tiles, LANES), li_residue.reshape(tiles, LANES), attn_query, attn_key,
    )


def choose(*args):
    n = lax.axis_size("seq")
    rows, chans = args[2].shape
    groups, mr_taps = args[7].shape
    modes = args[10].shape[1]
    fits = (
        chans % (n * LANES) == 0
        and HEAD_DIM == LANES
        and rows == 2 * mr_taps
        and mr_taps == LANES
        and chans // groups == modes
        and modes == HALO
        and args[4].shape[1] <= HALO
        and n > 1
    )
    return by_heads(*args) if fits else local(*args)


def solution(mesh):
    in_specs = (
        P("seq"),
        P(None, "chan"),
        P("seq", "chan"),
        P("seq", "chan"),
        P("chan", None),
        P("seq", "chan"),
        P("seq", "chan"),
        P("chan", None),
        P("seq", "chan"),
        P("seq", "chan"),
        P("chan", None),
        P("chan", None),
        P("seq", "chan"),
        P("seq", "chan"),
    )
    out_specs = P("seq", "chan")
    return jax.shard_map(choose, mesh=mesh, in_specs=in_specs, out_specs=out_specs, check_vma=False)
```

```python
import functools
import jax
import jax.numpy as jnp
from jax import lax
from jax.experimental import pallas as pl
from jax.experimental.pallas import tpu as pltpu
from jax.sharding import PartitionSpec as P

HEAD_DIM = 128


HIGHEST = lax.Precision.HIGHEST


def from_behind(block, axis, distance):
    devices = range(lax.axis_size(axis))
    route = [(i - distance, i) for i in devices if i - distance in devices]
    return lax.ppermute(block, axis, route)


def carried_in(value, axis, combine, identity):
    count, here = (lax.axis_size(axis), lax.axis_index(axis))
    everything = jax.tree.map(lambda part: lax.all_gather(part, axis), value)
    start = jax.tree.map(
        lambda part, zero: jnp.broadcast_to(jnp.asarray(zero, part.dtype), part.shape),
        value,
        identity,
    )

    def step(k, before):
        reached = k < here
        new = combine(before, jax.tree.map(lambda part: part[k], everything))
        return jax.tree.map(lambda a, b: jnp.where(reached, a, b), new, before)

    return lax.fori_loop(0, count, step, start)


def toeplitz_tables(filters, taps):
    lag_grid = (
        jnp.arange(taps, dtype=jnp.int32)[:, None] - jnp.arange(taps, dtype=jnp.int32)[None, :]
    )
    tap_ids = jnp.arange(taps, dtype=jnp.int32)[:, None, None]
    near_select = (lag_grid[None] == tap_ids).astype(jnp.float32)
    far_select = ((lag_grid + taps)[None] == tap_ids).astype(jnp.float32)
    filters_f = filters.astype(jnp.float32)
    current = jnp.einsum("gk,kts->gts", filters_f, near_select, precision=HIGHEST)
    previous = jnp.einsum("gk,kts->gts", filters_f, far_select, precision=HIGHEST)
    return (current, previous)


def local(
    token_ids,
    embed_table,
    se_query,
    se_key,
    se_filter,
    mr_query,
    mr_key,
    mr_filter,
    li_query,
    li_key,
    li_rate,
    li_residue,
    attn_query,
    attn_key,
):
    f32 = jnp.float32
    bf16 = jnp.bfloat16
    row_count = token_ids.shape[0]
    channels = embed_table.shape[1]
    group_count = se_filter.shape[0]
    group_width = channels // group_count
    seq_count = lax.axis_size("seq")
    chan_count = lax.axis_size("chan")
    total_len = row_count * seq_count
    vocab_ids = jnp.arange(embed_table.shape[0], dtype=jnp.int32)
    one_hot = (token_ids[:, None] == vocab_ids[None, :]).astype(bf16)
    stream = jnp.dot(one_hot, embed_table, preferred_element_type=f32).astype(bf16)
    se_taps = se_filter.shape[1]
    se_input = (se_key.astype(f32) * stream.astype(f32)).astype(bf16)
    se_edge = from_behind(se_input[row_count - (se_taps - 1) :], "seq", 1)
    se_padded = jnp.concatenate([se_edge, se_input], 0)
    tap_weights = jnp.repeat(se_filter.astype(f32), group_width, axis=0)
    se_conv = jnp.zeros((row_count, channels), f32)
    for tap_index in range(se_taps):
        start_row = se_taps - 1 - tap_index
        se_conv = (
            se_conv
            + se_padded[start_row : start_row + row_count].astype(f32) * tap_weights[:, tap_index]
        )
    stream = (stream.astype(f32) + se_query.astype(f32) * se_conv).astype(bf16)
    mr_taps = mr_filter.shape[1]
    mr_input = (mr_key.astype(f32) * stream.astype(f32)).astype(bf16)
    mr_edge = from_behind(mr_input[row_count - (mr_taps - 1) :], "seq", 1)
    block_count = row_count // mr_taps
    extended = jnp.concatenate([jnp.zeros((1, channels), bf16), mr_edge, mr_input], 0)
    extended = extended.reshape(block_count + 1, mr_taps, group_count, group_width)
    current_f, previous_f = toeplitz_tables(mr_filter, mr_taps)
    current = current_f.astype(bf16)
    previous = previous_f.astype(bf16)
    mr_conv = jnp.einsum("gts,bsgc->btgc", current, extended[1:], preferred_element_type=f32)
    mr_conv = mr_conv + jnp.einsum(
        "gts,bsgc->btgc", previous, extended[:-1], preferred_element_type=f32
    )
    stream = (
        stream.astype(f32) + mr_query.astype(f32) * mr_conv.reshape(row_count, channels)
    ).astype(bf16)
    li_input = (li_key.astype(f32) * stream.astype(f32)).astype(bf16)
    gain = li_residue * jnp.sqrt(1.0 - jnp.exp(-2.0 * li_rate) + 1.0 / total_len)
    lag_values = jnp.arange(mr_taps, dtype=f32)
    kernel_rows = jnp.sum(gain[:, :, None] * jnp.exp(-li_rate[:, :, None] * lag_values), axis=1)
    intra, unused_far = toeplitz_tables(kernel_rows, mr_taps)
    blocks_f = li_input.astype(f32).reshape(block_count, mr_taps, group_count, group_width)
    local_conv = jnp.einsum("gts,bsgc->btgc", intra, blocks_f, precision=HIGHEST)
    to_end = jnp.exp(-li_rate[:, :, None] * (mr_taps - 1 - lag_values))
    block_states = jnp.einsum("gms,bsgc->bmgc", to_end, blocks_f, precision=HIGHEST)
    block_ids = jnp.arange(block_count, dtype=f32)
    tail_decay = jnp.exp(-li_rate[None] * (mr_taps * (block_count - 1 - block_ids))[:, None, None])
    shard_state = jnp.einsum("bgm,bmgc->mgc", tail_decay, block_states, precision=HIGHEST)
    rate_column = li_rate.T[:, :, None]
    shard_decay = jnp.exp(-rate_column * row_count)

    def combine(earlier, later):
        return (earlier[0] * later[0], earlier[1] * later[0] + later[1])

    prefix = carried_in(
        (shard_decay, shard_state),
        "seq",
        combine,
        (jnp.ones_like(shard_decay), jnp.zeros_like(shard_state)),
    )
    carry_in = prefix[1]
    block_lag = block_ids[:, None] - 1.0 - block_ids[None, :]
    mixing = jnp.exp(
        -li_rate[None, None] * (mr_taps * jnp.maximum(block_lag, 0.0))[:, :, None, None]
    )
    mixing = jnp.where(block_lag[:, :, None, None] >= 0, mixing, 0.0)
    lead_decay = jnp.exp(-li_rate[None] * (mr_taps * block_ids)[:, None, None])
    block_carry = jnp.einsum("bdgm,dmgc->bmgc", mixing, block_states, precision=HIGHEST)
    block_carry = block_carry + jnp.einsum("bgm,mgc->bmgc", lead_decay, carry_in, precision=HIGHEST)
    emit = gain[:, None, :] * jnp.exp(-li_rate[:, None, :] * (lag_values + 1.0)[None, :, None])
    carry_conv = jnp.einsum("gtm,bmgc->btgc", emit, block_carry, precision=HIGHEST)
    li_conv = (local_conv + carry_conv).reshape(row_count, channels)
    stream = (stream.astype(f32) + li_query.astype(f32) * li_conv).astype(bf16)
    head_dim = HEAD_DIM
    local_heads = channels // head_dim
    part_rows = row_count // chan_count
    chan_index = lax.axis_index("chan")
    queries = attn_query.reshape(row_count, local_heads, head_dim)
    keys_local = attn_key.reshape(row_count, local_heads, head_dim)
    values_local = stream.reshape(row_count, local_heads, head_dim)
    q_heads, k_heads, v_heads = (
        lax.all_to_all(
            lax.all_to_all(queries, "chan", split_axis=0, concat_axis=1, tiled=True),
            "seq",
            split_axis=1,
            concat_axis=0,
            tiled=True,
        ),
        lax.all_to_all(
            lax.all_to_all(keys_local, "chan", split_axis=0, concat_axis=1, tiled=True),
            "seq",
            split_axis=1,
            concat_axis=0,
            tiled=True,
        ),
        lax.all_to_all(
            lax.all_to_all(values_local, "chan", split_axis=0, concat_axis=1, tiled=True),
            "seq",
            split_axis=1,
            concat_axis=0,
            tiled=True,
        ),
    )
    k_all, v_all = (
        lax.all_gather(k_heads, "chan", axis=0, tiled=True),
        lax.all_gather(v_heads, "chan", axis=0, tiled=True),
    )
    key_index = jnp.arange(chan_count * seq_count * part_rows, dtype=jnp.int32)
    key_chan = key_index // (seq_count * part_rows)
    key_rest = key_index % (seq_count * part_rows)
    key_pos = key_rest // part_rows * row_count + key_chan * part_rows + key_rest % part_rows
    query_count = q_heads.shape[0]
    head_count = q_heads.shape[1]
    query_index = jnp.arange(query_count, dtype=jnp.int32)
    query_pos = (
        query_index // part_rows * row_count + chan_index * part_rows + query_index % part_rows
    )
    block_rows = 512
    scale = head_dim ** (-0.5)

    def attend_block(packed):
        query_block, pos_block = packed
        scores = jnp.einsum("qhd,khd->hqk", query_block, k_all, preferred_element_type=f32) * scale
        allowed = key_pos[None, :] <= pos_block[:, None]
        scores = jnp.where(allowed[None], scores, -1e30)
        peak = jnp.max(scores, axis=2, keepdims=True)
        weights = jnp.where(allowed[None], jnp.exp(scores - peak), 0.0)
        totals = jnp.sum(weights, axis=2)
        mixed = jnp.einsum("hqk,khd->qhd", weights.astype(bf16), v_all, preferred_element_type=f32)
        return (mixed / totals.T[:, :, None]).astype(bf16)

    attended = lax.map(
        attend_block,
        (
            q_heads.reshape(query_count // block_rows, block_rows, head_count, head_dim),
            query_pos.reshape(query_count // block_rows, block_rows),
        ),
    )
    attended = attended.reshape(query_count, head_count, head_dim)
    returned = lax.all_to_all(
        lax.all_to_all(attended, "seq", split_axis=0, concat_axis=1, tiled=True),
        "chan",
        split_axis=1,
        concat_axis=0,
        tiled=True,
    )
    return (stream.astype(f32) + returned.reshape(row_count, channels).astype(f32)).astype(bf16)


LANES = 128
HALO = 16
MESH = pl.DeviceIdType.MESH


def fused(
    n, total_len,
    ids_ref, table_ref, sq_ref, sk_ref, sw_ref, mq_ref, mk_ref, mf_ref, lq_ref, lk_ref,
    rate_ref, res_ref, q_hbm, k_hbm, out_hbm,
    st, xs, hs, hx, mx, lx, lc, wt, s_mine, s_all, qh, kh, vh, ob, vb, sc, pw, tot,
    qss, qrs, kss, krs, vss, vrs, oss, ors, hss, hrs, sss, srs, own,
):
    f32, bf16 = jnp.float32, jnp.bfloat16
    me = lax.axis_index("seq")
    rows, chans = sq_ref.shape
    tiles = chans // LANES
    width = chans // n
    per = width // LANES
    half = rows // 2
    groups = mf_ref.shape[0]
    gpt = groups // tiles
    gw = LANES // gpt
    modes = LANES // gpt
    taps = sw_ref.shape[0]

    def lanes(start, size):
        return pl.ds(pl.multiple_of(start, LANES), size)

    def block(i):
        return pl.ds(pl.multiple_of(i * rows, rows), rows)

    barrier = pltpu.get_barrier_semaphore()

    def greet(i, c):
        pl.semaphore_signal(
            barrier, inc=1, device_id={"seq": lax.rem(me + i, n)}, device_id_type=MESH
        )
        return c

    lax.fori_loop(1, n, greet, 0)
    pl.semaphore_wait(barrier, n - 1)

    def spread(src, dst, ss, rs, peer, owner):
        return pltpu.make_async_remote_copy(
            src_ref=src.at[:, lanes(peer * width, width)],
            dst_ref=dst.at[block(owner), :],
            send_sem=ss.at[peer], recv_sem=rs.at[owner],
            device_id={"seq": peer}, device_id_type=MESH,
        )

    def give_back(peer, owner):
        return pltpu.make_async_remote_copy(
            src_ref=ob.at[block(peer), :],
            dst_ref=out_hbm.at[:, lanes(owner * width, width)],
            send_sem=oss.at[peer], recv_sem=ors.at[owner],
            device_id={"seq": peer}, device_id_type=MESH,
        )

    def state_copy(peer, owner):
        return pltpu.make_async_remote_copy(
            src_ref=s_mine, dst_ref=s_all.at[owner],
            send_sem=sss.at[peer], recv_sem=srs.at[owner],
            device_id={"seq": peer}, device_id_type=MESH,
        )

    nxt = lax.rem(me + 1, n)
    se_halo = pltpu.make_async_remote_copy(
        src_ref=hs, dst_ref=hx, send_sem=hss.at[0], recv_sem=hrs.at[0],
        device_id={"seq": nxt}, device_id_type=MESH,
    )
    mr_halo = pltpu.make_async_remote_copy(
        src_ref=mx.at[pl.ds(rows, half), :], dst_ref=mx.at[pl.ds(0, half), :],
        send_sem=hss.at[1], recv_sem=hrs.at[1],
        device_id={"seq": nxt}, device_id_type=MESH,
    )

    def send_all(src, dst, ss, rs):
        def one(i, c):
            spread(src, dst, ss, rs, lax.rem(me + i, n), me).start()
            return c

        lax.fori_loop(1, n, one, 0)

    own_q = pltpu.make_async_copy(q_hbm.at[:, lanes(me * width, width)], qh.at[block(me), :], own.at[0])
    own_k = pltpu.make_async_copy(k_hbm.at[:, lanes(me * width, width)], kh.at[block(me), :], own.at[1])
    own_q.start()
    own_k.start()

    def iota(shape, dim):
        return lax.broadcasted_iota(jnp.int32, shape, dim)

    vocab = table_ref.shape[0]
    ids_row = jnp.broadcast_to(ids_ref[...], (rows, rows))
    eye = iota((rows, rows), 0) == iota((rows, rows), 1)
    ids_col = jnp.sum(jnp.where(eye, ids_row, 0.0), axis=1, keepdims=True).astype(jnp.int32)
    one_hot = (iota((rows, vocab), 1) == ids_col).astype(f32).astype(bf16)

    def embed(j, c):
        at = lanes(j * 2 * LANES, 2 * LANES)
        e = jnp.dot(one_hot, table_ref[:, at], preferred_element_type=f32)
        st[:, at] = e.astype(bf16)
        gated = (sk_ref[:, at].astype(f32) * e).astype(bf16)
        xs[pl.ds(HALO, rows), at] = gated.astype(f32)
        hs[:, at] = gated[rows - HALO :, :]
        return c

    lax.fori_loop(0, tiles // 2, embed, 0)

    @pl.when(me < n - 1)
    def _():
        se_halo.start()

    send_all(q_hbm, qh, qss, qrs)

    @pl.when(me > 0)
    def _():
        se_halo.wait_recv()

    @pl.when(me == 0)
    def _():
        hx[...] = jnp.zeros_like(hx)
        mx[pl.ds(0, half), :] = jnp.zeros((half, chans), bf16)

    def short(j, c):
        at = lanes(j * LANES, LANES)
        xs[pl.ds(0, HALO), at] = hx[:, at].astype(f32)
        conv = jnp.zeros((rows, LANES), f32)
        for k in range(taps):
            conv = conv + xs[pl.ds(HALO - k, rows), at] * sw_ref[pl.ds(k, 1), at]
        s1 = (st[:, at].astype(f32) + sq_ref[:, at].astype(f32) * conv).astype(bf16)
        st[:, at] = s1
        mx[pl.ds(half, rows), at] = (mk_ref[:, at].astype(f32) * s1.astype(f32)).astype(bf16)
        return c

    lax.fori_loop(0, tiles, short, 0)

    @pl.when(me < n - 1)
    def _():
        mr_halo.start()


    @pl.when(me > 0)
    def _():
        mr_halo.wait_recv()

    eye_l = iota((LANES, LANES), 0) == iota((LANES, LANES), 1)
    lane_group = iota((half, 2 * LANES), 1) % LANES // gw
    back = (rows - 1 - iota((LANES, rows), 1)).astype(f32)
    causal = iota((half, rows), 1) <= iota((half, rows), 0) + half

    def column(row):
        return jnp.sum(
            jnp.where(eye_l, jnp.broadcast_to(row, (LANES, LANES)), 0.0), axis=1, keepdims=True
        )

    def gain_of(j):
        rate = rate_ref[pl.ds(j, 1), :]
        return rate, res_ref[pl.ds(j, 1), :] * jnp.sqrt(
            1.0 - jnp.exp(-2.0 * rate) + 1.0 / total_len
        )

    def pick(values, height, lg):
        acc = values[0:height, :]
        for g in range(1, gpt):
            acc = jnp.where(lg == g, values[g * height : (g + 1) * height, :], acc)
        return acc

    def toeplitz(kernels, mask):
        for g in range(gpt):
            wide = jnp.broadcast_to(kernels[g : g + 1, :], (half, rows))
            rolled = pltpu.roll(wide, half + 1, 1, stride=1, stride_axis=0)
            if mask is not None:
                rolled = jnp.where(mask, rolled, 0.0)
            wt[pl.ds(g * half, half), :] = rolled.astype(bf16)

    def stack(acc):
        return jnp.concatenate([acc[:, :LANES], acc[:, LANES:]], axis=0)

    lane_group_m = iota((modes, LANES), 1) // gw

    def medium(j, c):
        at = lanes(j * LANES, LANES)
        toeplitz(mf_ref[pl.ds(pl.multiple_of(j * gpt, gpt), gpt), :], None)
        both = jnp.concatenate([mx[pl.ds(0, rows), at], mx[pl.ds(half, rows), at]], axis=1)
        conv = stack(
            pick(jnp.dot(wt[...], both, preferred_element_type=f32), half, lane_group)
        )
        s2 = (st[:, at].astype(f32) + mq_ref[:, at].astype(f32) * conv).astype(bf16)
        st[:, at] = s2
        gated = (lk_ref[:, at].astype(f32) * s2.astype(f32)).astype(bf16)
        lx[:, at] = gated
        fade = jnp.exp(-column(rate_ref[pl.ds(j, 1), :]) * back).astype(bf16)
        ends = jnp.dot(fade, gated, preferred_element_type=f32)
        s_mine[:, at] = pick(ends, modes, lane_group_m).astype(bf16)
        return c

    lax.fori_loop(0, tiles, medium, 0)

    def push_state(p, c):
        state_copy(p, me).start()
        return c

    lax.fori_loop(me + 1, n, push_state, 0)
    send_all(k_hbm, kh, kss, krs)

    def long_local(j, c):
        at = lanes(j * LANES, LANES)
        rate, gain = gain_of(j)
        fade = jnp.exp(-column(rate) * back) * column(gain)
        toeplitz(jnp.sum(fade.reshape(gpt, modes, rows), axis=1), causal)
        x = lx[:, at]
        first = jnp.concatenate([jnp.zeros((half, LANES), bf16), x[:half, :]], axis=0)
        both = jnp.concatenate([first, x], axis=1)
        lc[:, at] = stack(
            pick(jnp.dot(wt[...], both, preferred_element_type=f32), half, lane_group)
        )
        return c

    lax.fori_loop(0, tiles, long_local, 0)

    def take_state(p, c):
        state_copy(me, p).wait_recv()
        return c

    lax.fori_loop(0, me, take_state, 0)

    after = (iota((rows, LANES), 0) + 1).astype(f32)
    same = iota((LANES, LANES), 0) // modes == iota((LANES, LANES), 1) // gw

    def long_carry(i, c):
        d = lax.rem(me + 1 + i, n)
        for u in range(per):
            j = d * per + u
            at = lanes(j * LANES, LANES)
            rate, gain = gain_of(j)
            rate_m = pick(jnp.broadcast_to(column(rate), (LANES, LANES)), modes, lane_group_m)
            decay = jnp.exp(-rate_m * float(rows))
            carry = lax.fori_loop(
                0, me, lambda p, s: s * decay + s_all[p, :, at].astype(f32),
                jnp.zeros((modes, LANES), f32),
            )
            full = jnp.where(same, jnp.concatenate([carry] * gpt, axis=0), 0.0)
            high = full.astype(bf16)
            low = (full - high.astype(f32)).astype(bf16)
            emit = (gain * jnp.exp(-after * rate)).astype(bf16)
            conv = lc[:, at] + jnp.dot(
                jnp.concatenate([emit, emit], axis=1),
                jnp.concatenate([high, low], axis=0),
                preferred_element_type=f32,
            )
            vb[:, at] = (st[:, at].astype(f32) + lq_ref[:, at].astype(f32) * conv).astype(bf16)

        @pl.when(i < n - 1)
        def _():
            spread(vb, vh, vss, vrs, d, me).start()

        return c

    lax.fori_loop(0, n, long_carry, 0)
    own_v = pltpu.make_async_copy(vb.at[:, lanes(me * width, width)], vh.at[block(me), :], own.at[2])
    own_v.start()
    own_q.wait()
    own_k.wait()

    def arrived(i, c):
        p = lax.rem(me + n - i, n)
        spread(q_hbm, qh, qss, qrs, me, p).wait_recv()
        spread(k_hbm, kh, kss, krs, me, p).wait_recv()
        return c

    lax.fori_loop(1, n, arrived, 0)

    factor = HEAD_DIM ** (-0.5) * 1.4426950408889634
    below = iota((rows, rows), 1) <= iota((rows, rows), 0)
    heads = [slice(u * LANES, (u + 1) * LANES) for u in range(per)]

    def weigh(i, c):
        r = lax.rem(me + 1 + i, n)
        qs = [qh[block(r), cols] for cols in heads]

        def score(b, tops, masked):
            new = []
            for u in range(per):
                s = lax.dot_general(
                    qs[u], kh[block(b), heads[u]], (((1,), (1,)), ((), ())),
                    preferred_element_type=f32,
                ) * factor
                if masked:
                    s = jnp.where(below, s, -1e30)
                sc[u, :, block(b)] = s
                new.append(jnp.maximum(tops[u], jnp.maximum(s[:, :LANES], s[:, LANES:])))
            return tuple(new)

        tops = score(r, (jnp.full((rows, LANES), -1e30, f32),) * per, True)
        tops = lax.fori_loop(0, r, lambda b, t: score(b, t, False), tops)
        peaks = [jnp.max(t, axis=1, keepdims=True) for t in tops]

        def weight(b, sums):
            new = []
            for u in range(per):
                w = jnp.exp2(sc[u, :, block(b)] - peaks[u])
                pw[u, block(r), block(b)] = w.astype(bf16)
                new.append(sums[u] + (w[:, :LANES] + w[:, LANES:]))
            return tuple(new)

        sums = lax.fori_loop(0, r + 1, weight, (jnp.zeros((rows, LANES), f32),) * per)
        for u in range(per):
            tot[u, block(r), :] = jnp.broadcast_to(
                jnp.sum(sums[u], axis=1, keepdims=True), (rows, LANES)
            )
        return c

    lax.fori_loop(0, n, weigh, 0)
    own_v.wait()

    def values_in(i, c):
        spread(vb, vh, vss, vrs, me, lax.rem(me + n - i, n)).wait_recv()
        return c

    lax.fori_loop(1, n, values_in, 0)

    def attend(i, c):
        r = lax.rem(me + 1 + i, n)

        def mix(b, accs):
            return tuple(
                accs[u] + jnp.dot(
                    pw[u, block(r), block(b)], vh[block(b), heads[u]], preferred_element_type=f32
                )
                for u in range(per)
            )

        accs = lax.fori_loop(0, r + 1, mix, (jnp.zeros((rows, LANES), f32),) * per)
        for u in range(per):
            got = (accs[u] / tot[u, block(r), :]).astype(bf16)
            ob[block(r), heads[u]] = (
                vh[block(r), heads[u]].astype(f32) + got.astype(f32)
            ).astype(bf16)

        @pl.when(i < n - 1)
        def _():
            give_back(r, me).start()

        return c

    lax.fori_loop(0, n, attend, 0)
    own_o = pltpu.make_async_copy(ob.at[block(me), :], out_hbm.at[:, lanes(me * width, width)], own.at[3])
    own_o.start()

    @pl.when(me < n - 1)
    def _():
        se_halo.wait_send()
        mr_halo.wait_send()

    def sent_state(p, c):
        state_copy(p, me).wait_send()
        return c

    lax.fori_loop(me + 1, n, sent_state, 0)

    def finish(i, c):
        p = lax.rem(me + i, n)
        spread(q_hbm, qh, qss, qrs, p, me).wait_send()
        spread(k_hbm, kh, kss, krs, p, me).wait_send()
        spread(vb, vh, vss, vrs, p, me).wait_send()
        give_back(p, me).wait_send()
        give_back(me, p).wait_recv()
        return c

    lax.fori_loop(1, n, finish, 0)
    own_o.wait()


def by_heads(
    token_ids, embed_table, se_query, se_key, se_filter, mr_query, mr_key, mr_filter,
    li_query, li_key, li_rate, li_residue, attn_query, attn_key,
):
    f32, bf16 = jnp.float32, jnp.bfloat16
    n = lax.axis_size("seq")
    rows, chans = se_query.shape
    groups, mr_taps = mr_filter.shape
    tiles = chans // LANES
    width = chans // n
    group_width = chans // groups
    modes = li_rate.shape[1]
    short_taps = jnp.repeat(se_filter.astype(f32).T, group_width, axis=1)
    reversed_mr = jnp.concatenate(
        [jnp.zeros((groups, rows - mr_taps), f32), mr_filter.astype(f32)[:, ::-1]], axis=1
    )
    vmem = pl.BlockSpec(memory_space=pltpu.VMEM)
    anywhere = pl.BlockSpec(memory_space=pl.ANY)
    dma = pltpu.SemaphoreType.DMA
    return pl.pallas_call(
        functools.partial(fused, n, n * rows),
        out_shape=jax.ShapeDtypeStruct((rows, chans), bf16),
        in_specs=[vmem] * 12 + [anywhere] * 2,
        out_specs=anywhere,
        scratch_shapes=[
            pltpu.VMEM((rows, chans), bf16),
            pltpu.VMEM((rows + HALO, chans), f32),
            pltpu.VMEM((HALO, chans), bf16),
            pltpu.VMEM((HALO, chans), bf16),
            pltpu.VMEM((rows + rows // 2, chans), bf16),
            pltpu.VMEM((rows, chans), bf16),
            pltpu.VMEM((rows, chans), f32),
            pltpu.VMEM((groups // tiles * rows // 2, rows), bf16),
            pltpu.VMEM((modes, chans), bf16),
            pltpu.VMEM((n, modes, chans), bf16),
            pltpu.VMEM((n * rows, width), bf16),
            pltpu.VMEM((n * rows, width), bf16),
            pltpu.VMEM((n * rows, width), bf16),
            pltpu.VMEM((n * rows, width), bf16),
            pltpu.VMEM((rows, chans), bf16),
            pltpu.VMEM((width // LANES, rows, n * rows), f32),
            pltpu.VMEM((width // LANES, n * rows, n * rows), bf16),
            pltpu.VMEM((width // LANES, n * rows, LANES), f32),
        ]
        + [dma((n,))] * 8 + [dma((2,))] * 2 + [dma((n,))] * 2 + [dma((4,))],
        compiler_params=pltpu.CompilerParams(
            collective_id=0, has_side_effects=True, vmem_limit_bytes=58 * 2**20
        ),
    )(
        token_ids.astype(f32).reshape(1, rows), embed_table, se_query, se_key, short_taps,
        mr_query, mr_key, reversed_mr, li_query, li_key,
        li_rate.reshape(tiles, LANES), li_residue.reshape(tiles, LANES), attn_query, attn_key,
    )


def choose(*args):
    n = lax.axis_size("seq")
    rows, chans = args[2].shape
    groups, mr_taps = args[7].shape
    modes = args[10].shape[1]
    fits = (
        chans % (n * LANES) == 0
        and HEAD_DIM == LANES
        and rows == 2 * mr_taps
        and mr_taps == LANES
        and chans // groups == modes
        and modes == HALO
        and args[4].shape[1] <= HALO
        and n > 1
    )
    return by_heads(*args) if fits else local(*args)


def solution(mesh):
    in_specs = (
        P("seq"),
        P(None, "chan"),
        P("seq", "chan"),
        P("seq", "chan"),
        P("chan", None),
        P("seq", "chan"),
        P("seq", "chan"),
        P("chan", None),
        P("seq", "chan"),
        P("seq", "chan"),
        P("chan", None),
        P("chan", None),
        P("seq", "chan"),
        P("seq", "chan"),
    )
    out_specs = P("seq", "chan")
    return jax.shard_map(choose, mesh=mesh, in_specs=in_specs, out_specs=out_specs, check_vma=False)
```

```python
import functools
import jax
import jax.numpy as jnp
from jax import lax
from jax.experimental import pallas as pl
from jax.experimental.pallas import tpu as pltpu
from jax.sharding import PartitionSpec as P

HEAD_DIM = 128


HIGHEST = lax.Precision.HIGHEST


def from_behind(block, axis, distance):
    devices = range(lax.axis_size(axis))
    route = [(i - distance, i) for i in devices if i - distance in devices]
    return lax.ppermute(block, axis, route)


def carried_in(value, axis, combine, identity):
    count, here = (lax.axis_size(axis), lax.axis_index(axis))
    everything = jax.tree.map(lambda part: lax.all_gather(part, axis), value)
    start = jax.tree.map(
        lambda part, zero: jnp.broadcast_to(jnp.asarray(zero, part.dtype), part.shape),
        value,
        identity,
    )

    def step(k, before):
        reached = k < here
        new = combine(before, jax.tree.map(lambda part: part[k], everything))
        return jax.tree.map(lambda a, b: jnp.where(reached, a, b), new, before)

    return lax.fori_loop(0, count, step, start)


def toeplitz_tables(filters, taps):
    lag_grid = (
        jnp.arange(taps, dtype=jnp.int32)[:, None] - jnp.arange(taps, dtype=jnp.int32)[None, :]
    )
    tap_ids = jnp.arange(taps, dtype=jnp.int32)[:, None, None]
    near_select = (lag_grid[None] == tap_ids).astype(jnp.float32)
    far_select = ((lag_grid + taps)[None] == tap_ids).astype(jnp.float32)
    filters_f = filters.astype(jnp.float32)
    current = jnp.einsum("gk,kts->gts", filters_f, near_select, precision=HIGHEST)
    previous = jnp.einsum("gk,kts->gts", filters_f, far_select, precision=HIGHEST)
    return (current, previous)


def local(
    token_ids,
    embed_table,
    se_query,
    se_key,
    se_filter,
    mr_query,
    mr_key,
    mr_filter,
    li_query,
    li_key,
    li_rate,
    li_residue,
    attn_query,
    attn_key,
):
    f32 = jnp.float32
    bf16 = jnp.bfloat16
    row_count = token_ids.shape[0]
    channels = embed_table.shape[1]
    group_count = se_filter.shape[0]
    group_width = channels // group_count
    seq_count = lax.axis_size("seq")
    chan_count = lax.axis_size("chan")
    total_len = row_count * seq_count
    vocab_ids = jnp.arange(embed_table.shape[0], dtype=jnp.int32)
    one_hot = (token_ids[:, None] == vocab_ids[None, :]).astype(bf16)
    stream = jnp.dot(one_hot, embed_table, preferred_element_type=f32).astype(bf16)
    se_taps = se_filter.shape[1]
    se_input = (se_key.astype(f32) * stream.astype(f32)).astype(bf16)
    se_edge = from_behind(se_input[row_count - (se_taps - 1) :], "seq", 1)
    se_padded = jnp.concatenate([se_edge, se_input], 0)
    tap_weights = jnp.repeat(se_filter.astype(f32), group_width, axis=0)
    se_conv = jnp.zeros((row_count, channels), f32)
    for tap_index in range(se_taps):
        start_row = se_taps - 1 - tap_index
        se_conv = (
            se_conv
            + se_padded[start_row : start_row + row_count].astype(f32) * tap_weights[:, tap_index]
        )
    stream = (stream.astype(f32) + se_query.astype(f32) * se_conv).astype(bf16)
    mr_taps = mr_filter.shape[1]
    mr_input = (mr_key.astype(f32) * stream.astype(f32)).astype(bf16)
    mr_edge = from_behind(mr_input[row_count - (mr_taps - 1) :], "seq", 1)
    block_count = row_count // mr_taps
    extended = jnp.concatenate([jnp.zeros((1, channels), bf16), mr_edge, mr_input], 0)
    extended = extended.reshape(block_count + 1, mr_taps, group_count, group_width)
    current_f, previous_f = toeplitz_tables(mr_filter, mr_taps)
    current = current_f.astype(bf16)
    previous = previous_f.astype(bf16)
    mr_conv = jnp.einsum("gts,bsgc->btgc", current, extended[1:], preferred_element_type=f32)
    mr_conv = mr_conv + jnp.einsum(
        "gts,bsgc->btgc", previous, extended[:-1], preferred_element_type=f32
    )
    stream = (
        stream.astype(f32) + mr_query.astype(f32) * mr_conv.reshape(row_count, channels)
    ).astype(bf16)
    li_input = (li_key.astype(f32) * stream.astype(f32)).astype(bf16)
    gain = li_residue * jnp.sqrt(1.0 - jnp.exp(-2.0 * li_rate) + 1.0 / total_len)
    lag_values = jnp.arange(mr_taps, dtype=f32)
    kernel_rows = jnp.sum(gain[:, :, None] * jnp.exp(-li_rate[:, :, None] * lag_values), axis=1)
    intra, unused_far = toeplitz_tables(kernel_rows, mr_taps)
    blocks_f = li_input.astype(f32).reshape(block_count, mr_taps, group_count, group_width)
    local_conv = jnp.einsum("gts,bsgc->btgc", intra, blocks_f, precision=HIGHEST)
    to_end = jnp.exp(-li_rate[:, :, None] * (mr_taps - 1 - lag_values))
    block_states = jnp.einsum("gms,bsgc->bmgc", to_end, blocks_f, precision=HIGHEST)
    block_ids = jnp.arange(block_count, dtype=f32)
    tail_decay = jnp.exp(-li_rate[None] * (mr_taps * (block_count - 1 - block_ids))[:, None, None])
    shard_state = jnp.einsum("bgm,bmgc->mgc", tail_decay, block_states, precision=HIGHEST)
    rate_column = li_rate.T[:, :, None]
    shard_decay = jnp.exp(-rate_column * row_count)

    def combine(earlier, later):
        return (earlier[0] * later[0], earlier[1] * later[0] + later[1])

    prefix = carried_in(
        (shard_decay, shard_state),
        "seq",
        combine,
        (jnp.ones_like(shard_decay), jnp.zeros_like(shard_state)),
    )
    carry_in = prefix[1]
    block_lag = block_ids[:, None] - 1.0 - block_ids[None, :]
    mixing = jnp.exp(
        -li_rate[None, None] * (mr_taps * jnp.maximum(block_lag, 0.0))[:, :, None, None]
    )
    mixing = jnp.where(block_lag[:, :, None, None] >= 0, mixing, 0.0)
    lead_decay = jnp.exp(-li_rate[None] * (mr_taps * block_ids)[:, None, None])
    block_carry = jnp.einsum("bdgm,dmgc->bmgc", mixing, block_states, precision=HIGHEST)
    block_carry = block_carry + jnp.einsum("bgm,mgc->bmgc", lead_decay, carry_in, precision=HIGHEST)
    emit = gain[:, None, :] * jnp.exp(-li_rate[:, None, :] * (lag_values + 1.0)[None, :, None])
    carry_conv = jnp.einsum("gtm,bmgc->btgc", emit, block_carry, precision=HIGHEST)
    li_conv = (local_conv + carry_conv).reshape(row_count, channels)
    stream = (stream.astype(f32) + li_query.astype(f32) * li_conv).astype(bf16)
    head_dim = HEAD_DIM
    local_heads = channels // head_dim
    part_rows = row_count // chan_count
    chan_index = lax.axis_index("chan")
    queries = attn_query.reshape(row_count, local_heads, head_dim)
    keys_local = attn_key.reshape(row_count, local_heads, head_dim)
    values_local = stream.reshape(row_count, local_heads, head_dim)
    q_heads, k_heads, v_heads = (
        lax.all_to_all(
            lax.all_to_all(queries, "chan", split_axis=0, concat_axis=1, tiled=True),
            "seq",
            split_axis=1,
            concat_axis=0,
            tiled=True,
        ),
        lax.all_to_all(
            lax.all_to_all(keys_local, "chan", split_axis=0, concat_axis=1, tiled=True),
            "seq",
            split_axis=1,
            concat_axis=0,
            tiled=True,
        ),
        lax.all_to_all(
            lax.all_to_all(values_local, "chan", split_axis=0, concat_axis=1, tiled=True),
            "seq",
            split_axis=1,
            concat_axis=0,
            tiled=True,
        ),
    )
    k_all, v_all = (
        lax.all_gather(k_heads, "chan", axis=0, tiled=True),
        lax.all_gather(v_heads, "chan", axis=0, tiled=True),
    )
    key_index = jnp.arange(chan_count * seq_count * part_rows, dtype=jnp.int32)
    key_chan = key_index // (seq_count * part_rows)
    key_rest = key_index % (seq_count * part_rows)
    key_pos = key_rest // part_rows * row_count + key_chan * part_rows + key_rest % part_rows
    query_count = q_heads.shape[0]
    head_count = q_heads.shape[1]
    query_index = jnp.arange(query_count, dtype=jnp.int32)
    query_pos = (
        query_index // part_rows * row_count + chan_index * part_rows + query_index % part_rows
    )
    block_rows = 512
    scale = head_dim ** (-0.5)

    def attend_block(packed):
        query_block, pos_block = packed
        scores = jnp.einsum("qhd,khd->hqk", query_block, k_all, preferred_element_type=f32) * scale
        allowed = key_pos[None, :] <= pos_block[:, None]
        scores = jnp.where(allowed[None], scores, -1e30)
        peak = jnp.max(scores, axis=2, keepdims=True)
        weights = jnp.where(allowed[None], jnp.exp(scores - peak), 0.0)
        totals = jnp.sum(weights, axis=2)
        mixed = jnp.einsum("hqk,khd->qhd", weights.astype(bf16), v_all, preferred_element_type=f32)
        return (mixed / totals.T[:, :, None]).astype(bf16)

    attended = lax.map(
        attend_block,
        (
            q_heads.reshape(query_count // block_rows, block_rows, head_count, head_dim),
            query_pos.reshape(query_count // block_rows, block_rows),
        ),
    )
    attended = attended.reshape(query_count, head_count, head_dim)
    returned = lax.all_to_all(
        lax.all_to_all(attended, "seq", split_axis=0, concat_axis=1, tiled=True),
        "chan",
        split_axis=1,
        concat_axis=0,
        tiled=True,
    )
    return (stream.astype(f32) + returned.reshape(row_count, channels).astype(f32)).astype(bf16)


LANES = 128
HALO = 16
MESH = pl.DeviceIdType.MESH


def fused(
    n, total_len,
    ids_ref, table_ref, sq_ref, sk_ref, sw_ref, mq_ref, mk_ref, mf_ref, lq_ref, lk_ref,
    rate_ref, res_ref, q_hbm, k_hbm, out_hbm,
    st, xs, hs, hx, mx, lx, lc, wt, s_mine, s_all, qh, kh, vh, ob, vb, sc, pw, tot,
    qss, qrs, kss, krs, vss, vrs, oss, ors, hss, hrs, sss, srs, own,
):
    f32, bf16 = jnp.float32, jnp.bfloat16
    me = lax.axis_index("seq")
    rows, chans = sq_ref.shape
    tiles = chans // LANES
    width = chans // n
    per = width // LANES
    half = rows // 2
    groups = mf_ref.shape[0]
    gpt = groups // tiles
    gw = LANES // gpt
    modes = LANES // gpt
    taps = sw_ref.shape[0]

    def lanes(start, size):
        return pl.ds(pl.multiple_of(start, LANES), size)

    def block(i):
        return pl.ds(pl.multiple_of(i * rows, rows), rows)

    barrier = pltpu.get_barrier_semaphore()

    def greet(i, c):
        pl.semaphore_signal(
            barrier, inc=1, device_id={"seq": lax.rem(me + i, n)}, device_id_type=MESH
        )
        return c

    lax.fori_loop(1, n, greet, 0)
    pl.semaphore_wait(barrier, n - 1)

    def spread(src, dst, ss, rs, peer, owner):
        return pltpu.make_async_remote_copy(
            src_ref=src.at[:, lanes(peer * width, width)],
            dst_ref=dst.at[block(owner), :],
            send_sem=ss.at[peer], recv_sem=rs.at[owner],
            device_id={"seq": peer}, device_id_type=MESH,
        )

    def give_back(peer, owner):
        return pltpu.make_async_remote_copy(
            src_ref=ob.at[block(peer), :],
            dst_ref=out_hbm.at[:, lanes(owner * width, width)],
            send_sem=oss.at[peer], recv_sem=ors.at[owner],
            device_id={"seq": peer}, device_id_type=MESH,
        )

    def state_copy(peer, owner):
        return pltpu.make_async_remote_copy(
            src_ref=s_mine, dst_ref=s_all.at[owner],
            send_sem=sss.at[peer], recv_sem=srs.at[owner],
            device_id={"seq": peer}, device_id_type=MESH,
        )

    nxt = lax.rem(me + 1, n)
    se_halo = pltpu.make_async_remote_copy(
        src_ref=hs, dst_ref=hx, send_sem=hss.at[0], recv_sem=hrs.at[0],
        device_id={"seq": nxt}, device_id_type=MESH,
    )
    mr_halo = pltpu.make_async_remote_copy(
        src_ref=mx.at[pl.ds(rows, half), :], dst_ref=mx.at[pl.ds(0, half), :],
        send_sem=hss.at[1], recv_sem=hrs.at[1],
        device_id={"seq": nxt}, device_id_type=MESH,
    )

    def send_all(src, dst, ss, rs):
        def one(i, c):
            spread(src, dst, ss, rs, lax.rem(me + i, n), me).start()
            return c

        lax.fori_loop(1, n, one, 0)

    own_q = pltpu.make_async_copy(q_hbm.at[:, lanes(me * width, width)], qh.at[block(me), :], own.at[0])
    own_k = pltpu.make_async_copy(k_hbm.at[:, lanes(me * width, width)], kh.at[block(me), :], own.at[1])
    own_q.start()
    own_k.start()

    def iota(shape, dim):
        return lax.broadcasted_iota(jnp.int32, shape, dim)

    vocab = table_ref.shape[0]
    ids_row = jnp.broadcast_to(ids_ref[...], (rows, rows))
    eye = iota((rows, rows), 0) == iota((rows, rows), 1)
    ids_col = jnp.sum(jnp.where(eye, ids_row, 0.0), axis=1, keepdims=True).astype(jnp.int32)
    one_hot = (iota((rows, vocab), 1) == ids_col).astype(f32).astype(bf16)

    def embed(j, c):
        at = lanes(j * 2 * LANES, 2 * LANES)
        e = jnp.dot(one_hot, table_ref[:, at], preferred_element_type=f32)
        st[:, at] = e.astype(bf16)
        gated = (sk_ref[:, at].astype(f32) * e).astype(bf16)
        xs[pl.ds(HALO, rows), at] = gated.astype(f32)
        hs[:, at] = gated[rows - HALO :, :]
        return c

    lax.fori_loop(0, tiles // 2, embed, 0)

    @pl.when(me < n - 1)
    def _():
        se_halo.start()

    send_all(q_hbm, qh, qss, qrs)

    @pl.when(me > 0)
    def _():
        se_halo.wait_recv()

    @pl.when(me == 0)
    def _():
        hx[...] = jnp.zeros_like(hx)
        mx[pl.ds(0, half), :] = jnp.zeros((half, chans), bf16)

    def short(j, c):
        at = lanes(j * LANES, LANES)
        xs[pl.ds(0, HALO), at] = hx[:, at].astype(f32)
        conv = jnp.zeros((rows, LANES), f32)
        for k in range(taps):
            conv = conv + xs[pl.ds(HALO - k, rows), at] * sw_ref[pl.ds(k, 1), at]
        s1 = (st[:, at].astype(f32) + sq_ref[:, at].astype(f32) * conv).astype(bf16)
        st[:, at] = s1
        mx[pl.ds(half, rows), at] = (mk_ref[:, at].astype(f32) * s1.astype(f32)).astype(bf16)
        return c

    lax.fori_loop(0, tiles, short, 0)

    @pl.when(me < n - 1)
    def _():
        mr_halo.start()


    @pl.when(me > 0)
    def _():
        mr_halo.wait_recv()

    eye_l = iota((LANES, LANES), 0) == iota((LANES, LANES), 1)
    lane_group = iota((half, 2 * LANES), 1) % LANES // gw
    back = (rows - 1 - iota((LANES, rows), 1)).astype(f32)
    causal = iota((half, rows), 1) <= iota((half, rows), 0) + half

    def column(row):
        return jnp.sum(
            jnp.where(eye_l, jnp.broadcast_to(row, (LANES, LANES)), 0.0), axis=1, keepdims=True
        )

    def gain_of(j):
        rate = rate_ref[pl.ds(j, 1), :]
        return rate, res_ref[pl.ds(j, 1), :] * jnp.sqrt(
            1.0 - jnp.exp(-2.0 * rate) + 1.0 / total_len
        )

    def pick(values, height, lg):
        acc = values[0:height, :]
        for g in range(1, gpt):
            acc = jnp.where(lg == g, values[g * height : (g + 1) * height, :], acc)
        return acc

    def toeplitz(kernels, mask):
        for g in range(gpt):
            wide = jnp.broadcast_to(kernels[g : g + 1, :], (half, rows))
            rolled = pltpu.roll(wide, half + 1, 1, stride=1, stride_axis=0)
            if mask is not None:
                rolled = jnp.where(mask, rolled, 0.0)
            wt[pl.ds(g * half, half), :] = rolled.astype(bf16)

    def stack(acc):
        return jnp.concatenate([acc[:, :LANES], acc[:, LANES:]], axis=0)

    lane_group_m = iota((modes, LANES), 1) // gw

    def medium(j, c):
        at = lanes(j * LANES, LANES)
        toeplitz(mf_ref[pl.ds(pl.multiple_of(j * gpt, gpt), gpt), :], None)
        both = jnp.concatenate([mx[pl.ds(0, rows), at], mx[pl.ds(half, rows), at]], axis=1)
        conv = stack(
            pick(jnp.dot(wt[...], both, preferred_element_type=f32), half, lane_group)
        )
        s2 = (st[:, at].astype(f32) + mq_ref[:, at].astype(f32) * conv).astype(bf16)
        st[:, at] = s2
        gated = (lk_ref[:, at].astype(f32) * s2.astype(f32)).astype(bf16)
        lx[:, at] = gated
        fade = jnp.exp(-column(rate_ref[pl.ds(j, 1), :]) * back).astype(bf16)
        ends = jnp.dot(fade, gated, preferred_element_type=f32)
        s_mine[:, at] = pick(ends, modes, lane_group_m).astype(bf16)
        return c

    lax.fori_loop(0, tiles, medium, 0)

    def push_state(p, c):
        state_copy(p, me).start()
        return c

    lax.fori_loop(me + 1, n, push_state, 0)
    send_all(k_hbm, kh, kss, krs)

    def long_local(j, c):
        at = lanes(j * LANES, LANES)
        rate, gain = gain_of(j)
        fade = jnp.exp(-column(rate) * back) * column(gain)
        toeplitz(jnp.sum(fade.reshape(gpt, modes, rows), axis=1), causal)
        x = lx[:, at]
        first = jnp.concatenate([jnp.zeros((half, LANES), bf16), x[:half, :]], axis=0)
        both = jnp.concatenate([first, x], axis=1)
        lc[:, at] = stack(
            pick(jnp.dot(wt[...], both, preferred_element_type=f32), half, lane_group)
        )
        return c

    lax.fori_loop(0, tiles, long_local, 0)

    def take_state(p, c):
        state_copy(me, p).wait_recv()
        return c

    lax.fori_loop(0, me, take_state, 0)

    after = (iota((rows, LANES), 0) + 1).astype(f32)
    same = iota((LANES, LANES), 0) // modes == iota((LANES, LANES), 1) // gw

    def long_carry(i, c):
        d = lax.rem(me + 1 + i, n)
        for u in range(per):
            j = d * per + u
            at = lanes(j * LANES, LANES)
            rate, gain = gain_of(j)
            rate_m = pick(jnp.broadcast_to(column(rate), (LANES, LANES)), modes, lane_group_m)
            decay = jnp.exp(-rate_m * float(rows))
            carry = lax.fori_loop(
                0, me, lambda p, s: s * decay + s_all[p, :, at].astype(f32),
                jnp.zeros((modes, LANES), f32),
            )
            full = jnp.where(same, jnp.concatenate([carry] * gpt, axis=0), 0.0)
            high = full.astype(bf16)
            low = (full - high.astype(f32)).astype(bf16)
            emit = (gain * jnp.exp(-after * rate)).astype(bf16)
            conv = lc[:, at] + jnp.dot(
                jnp.concatenate([emit, emit], axis=1),
                jnp.concatenate([high, low], axis=0),
                preferred_element_type=f32,
            )
            vb[:, at] = (st[:, at].astype(f32) + lq_ref[:, at].astype(f32) * conv).astype(bf16)

        @pl.when(i < n - 1)
        def _():
            spread(vb, vh, vss, vrs, d, me).start()

        return c

    lax.fori_loop(0, n, long_carry, 0)
    own_v = pltpu.make_async_copy(vb.at[:, lanes(me * width, width)], vh.at[block(me), :], own.at[2])
    own_v.start()
    own_q.wait()
    own_k.wait()

    def arrived(i, c):
        p = lax.rem(me + n - i, n)
        spread(q_hbm, qh, qss, qrs, me, p).wait_recv()
        spread(k_hbm, kh, kss, krs, me, p).wait_recv()
        return c

    lax.fori_loop(1, n, arrived, 0)

    factor = HEAD_DIM ** (-0.5) * 1.4426950408889634
    below = iota((rows, rows), 1) <= iota((rows, rows), 0)
    heads = [slice(u * LANES, (u + 1) * LANES) for u in range(per)]

    def weigh(i, c):
        r = lax.rem(me + 1 + i, n)
        qs = [qh[block(r), cols] for cols in heads]

        def score(b, tops, masked):
            new = []
            for u in range(per):
                s = lax.dot_general(
                    qs[u], kh[block(b), heads[u]], (((1,), (1,)), ((), ())),
                    preferred_element_type=f32,
                ) * factor
                if masked:
                    s = jnp.where(below, s, -1e30)
                sc[u, :, block(b)] = s
                new.append(jnp.maximum(tops[u], jnp.maximum(s[:, :LANES], s[:, LANES:])))
            return tuple(new)

        tops = score(r, (jnp.full((rows, LANES), -1e30, f32),) * per, True)
        tops = lax.fori_loop(0, r, lambda b, t: score(b, t, False), tops)
        peaks = [jnp.max(t, axis=1, keepdims=True) for t in tops]

        def weight(b, sums):
            new = []
            for u in range(per):
                w = jnp.exp2(sc[u, :, block(b)] - peaks[u])
                pw[u, block(r), block(b)] = w.astype(bf16)
                new.append(sums[u] + (w[:, :LANES] + w[:, LANES:]))
            return tuple(new)

        sums = lax.fori_loop(0, r + 1, weight, (jnp.zeros((rows, LANES), f32),) * per)
        for u in range(per):
            tot[u, block(r), :] = jnp.broadcast_to(
                jnp.sum(sums[u], axis=1, keepdims=True), (rows, LANES)
            )
        return c

    lax.fori_loop(0, n, weigh, 0)
    own_v.wait()

    def values_in(i, c):
        spread(vb, vh, vss, vrs, me, i).wait_recv()
        return c

    lax.fori_loop(0, me, values_in, 0)

    def attend(i, c):
        r = lax.rem(me + 2 * n - 1 - i, n)

        @pl.when(i == me)
        def _():
            lax.fori_loop(me + 1, n, values_in, 0)

        def mix(b, accs):
            return tuple(
                accs[u] + jnp.dot(
                    pw[u, block(r), block(b)], vh[block(b), heads[u]], preferred_element_type=f32
                )
                for u in range(per)
            )

        accs = lax.fori_loop(0, r + 1, mix, (jnp.zeros((rows, LANES), f32),) * per)
        for u in range(per):
            got = (accs[u] / tot[u, block(r), :]).astype(bf16)
            ob[block(r), heads[u]] = (
                vh[block(r), heads[u]].astype(f32) + got.astype(f32)
            ).astype(bf16)

        @pl.when(i < n - 1)
        def _():
            give_back(r, me).start()

        return c

    lax.fori_loop(0, n, attend, 0)
    own_o = pltpu.make_async_copy(ob.at[block(me), :], out_hbm.at[:, lanes(me * width, width)], own.at[3])
    own_o.start()

    @pl.when(me < n - 1)
    def _():
        se_halo.wait_send()
        mr_halo.wait_send()

    def sent_state(p, c):
        state_copy(p, me).wait_send()
        return c

    lax.fori_loop(me + 1, n, sent_state, 0)

    def finish(i, c):
        p = lax.rem(me + i, n)
        spread(q_hbm, qh, qss, qrs, p, me).wait_send()
        spread(k_hbm, kh, kss, krs, p, me).wait_send()
        spread(vb, vh, vss, vrs, p, me).wait_send()
        give_back(p, me).wait_send()
        give_back(me, p).wait_recv()
        return c

    lax.fori_loop(1, n, finish, 0)
    own_o.wait()


def by_heads(
    token_ids, embed_table, se_query, se_key, se_filter, mr_query, mr_key, mr_filter,
    li_query, li_key, li_rate, li_residue, attn_query, attn_key,
):
    f32, bf16 = jnp.float32, jnp.bfloat16
    n = lax.axis_size("seq")
    rows, chans = se_query.shape
    groups, mr_taps = mr_filter.shape
    tiles = chans // LANES
    width = chans // n
    group_width = chans // groups
    modes = li_rate.shape[1]
    short_taps = jnp.repeat(se_filter.astype(f32).T, group_width, axis=1)
    reversed_mr = jnp.concatenate(
        [jnp.zeros((groups, rows - mr_taps), f32), mr_filter.astype(f32)[:, ::-1]], axis=1
    )
    vmem = pl.BlockSpec(memory_space=pltpu.VMEM)
    anywhere = pl.BlockSpec(memory_space=pl.ANY)
    dma = pltpu.SemaphoreType.DMA
    return pl.pallas_call(
        functools.partial(fused, n, n * rows),
        out_shape=jax.ShapeDtypeStruct((rows, chans), bf16),
        in_specs=[vmem] * 12 + [anywhere] * 2,
        out_specs=anywhere,
        scratch_shapes=[
            pltpu.VMEM((rows, chans), bf16),
            pltpu.VMEM((rows + HALO, chans), f32),
            pltpu.VMEM((HALO, chans), bf16),
            pltpu.VMEM((HALO, chans), bf16),
            pltpu.VMEM((rows + rows // 2, chans), bf16),
            pltpu.VMEM((rows, chans), bf16),
            pltpu.VMEM((rows, chans), f32),
            pltpu.VMEM((groups // tiles * rows // 2, rows), bf16),
            pltpu.VMEM((modes, chans), bf16),
            pltpu.VMEM((n, modes, chans), bf16),
            pltpu.VMEM((n * rows, width), bf16),
            pltpu.VMEM((n * rows, width), bf16),
            pltpu.VMEM((n * rows, width), bf16),
            pltpu.VMEM((n * rows, width), bf16),
            pltpu.VMEM((rows, chans), bf16),
            pltpu.VMEM((width // LANES, rows, n * rows), f32),
            pltpu.VMEM((width // LANES, n * rows, n * rows), bf16),
            pltpu.VMEM((width // LANES, n * rows, LANES), f32),
        ]
        + [dma((n,))] * 8 + [dma((2,))] * 2 + [dma((n,))] * 2 + [dma((4,))],
        compiler_params=pltpu.CompilerParams(
            collective_id=0, has_side_effects=True, vmem_limit_bytes=58 * 2**20
        ),
    )(
        token_ids.astype(f32).reshape(1, rows), embed_table, se_query, se_key, short_taps,
        mr_query, mr_key, reversed_mr, li_query, li_key,
        li_rate.reshape(tiles, LANES), li_residue.reshape(tiles, LANES), attn_query, attn_key,
    )


def choose(*args):
    n = lax.axis_size("seq")
    rows, chans = args[2].shape
    groups, mr_taps = args[7].shape
    modes = args[10].shape[1]
    fits = (
        chans % (n * LANES) == 0
        and HEAD_DIM == LANES
        and rows == 2 * mr_taps
        and mr_taps == LANES
        and chans // groups == modes
        and modes == HALO
        and args[4].shape[1] <= HALO
        and n > 1
    )
    return by_heads(*args) if fits else local(*args)


def solution(mesh):
    in_specs = (
        P("seq"),
        P(None, "chan"),
        P("seq", "chan"),
        P("seq", "chan"),
        P("chan", None),
        P("seq", "chan"),
        P("seq", "chan"),
        P("chan", None),
        P("seq", "chan"),
        P("seq", "chan"),
        P("chan", None),
        P("chan", None),
        P("seq", "chan"),
        P("seq", "chan"),
    )
    out_specs = P("seq", "chan")
    return jax.shard_map(choose, mesh=mesh, in_specs=in_specs, out_specs=out_specs, check_vma=False)
```
